256 devices in a mesh: seq: 16 (over x_lo, z), cfg: 16 (over y, x_hi, core).
Axes of the slice: x: 4 (x_hi: 2, x_lo: 2; x = x_hi * 2 + x_lo), y: 4, z: 8, core: 2. Of those that a mesh axis runs over, the one named last changes fastest.
Arguments:
- query_states: bfloat16 [16, 1536, 4096], P('cfg', 'seq'), may hold values from -8 to 8
- key_states: bfloat16 [16, 9216, 4096], P('cfg', 'seq'), may hold values from -8 to 8
- value_states: bfloat16 [16, 9216, 4096], P('cfg', 'seq'), may hold values from -6 to 6
- tile_pattern: int32 [8, 28], replicated, may hold values from -1 to 47, as said below
- strength: float32 [16], replicated, may hold values from 1 to 8
- partner: int32 [16], replicated, may hold values from 0 to 15, as said below
Outputs:
- guided: bfloat16 [16, 1536, 4096], P('cfg', 'seq')
The draws below stay inside these ranges and needn't reach their ends.
Inputs may be any that keep to these rules, and one draw needn't show every extreme that they name: `tile_pattern`: each row holds 27 distinct tile numbers, those of a block of 3 x 3 x 3 neighbouring tiles that contains the row's own tile, and one entry -1 at some position. partner[partner[m]] = m and partner[m] != m.
All inputs are finite; a program needn't handle non-finite values.
Results may differ from the reference program's by a relative error of at most 0.0057.
Values may be sent and summed in bfloat16 or wider, within the bound.
A program may use at most 128 MiB of HBM per device.

```python
import math
import jax
import jax.numpy as jnp
from jax import lax

HEADS = 32
HEAD_DIM = 128
TILE_T = 6
TILE_H = 8
TILE_W = 4
GT = 3
GH = 4
GW = 4
QUERY_TILES = 8
SLOTS = 28
TOKENS = 9216
QUERY_TOKENS = 1536
MEMBERS = 16


def draw_query_states(key, part):
    key = jax.random.fold_in(key, 3)
    second_key = jax.random.fold_in(key, 1)
    array_shape = (MEMBERS, QUERY_TOKENS, HEADS * HEAD_DIM)
    drawn = jnp.clip(jax.random.normal(second_key, array_shape), -8.0, 8.0)
    return drawn.astype(jnp.bfloat16)


def draw_key_states(key, part):
    key = jax.random.fold_in(key, 5)
    second_key = jax.random.fold_in(key, 1)
    array_shape = (MEMBERS, TOKENS, HEADS * HEAD_DIM)
    drawn = jnp.clip(jax.random.normal(second_key, array_shape), -8.0, 8.0)
    return drawn.astype(jnp.bfloat16)


def draw_tile_pattern(key, part):
    key = jax.random.fold_in(key, 7)
    shift_key, slot_key = jax.random.split(key)
    tile_ids = jnp.arange(QUERY_TILES)
    coord_w = tile_ids % GW
    coord_h = tile_ids // GW % GH
    coord_t = tile_ids // (GW * GH)
    shifts = jax.random.randint(shift_key, (QUERY_TILES, 3), -1, 2)
    start_t = jnp.clip(coord_t - 1 + shifts[:, 0], 0, GT - 3)
    start_h = jnp.clip(coord_h - 1 + shifts[:, 1], 0, GH - 3)
    start_w = jnp.clip(coord_w - 1 + shifts[:, 2], 0, GW - 3)
    corner = jnp.arange(27)
    reach_t = corner // 9
    reach_h = corner // 3 % 3
    reach_w = corner % 3
    window_tiles = ((start_t[:, None] + reach_t) * GH + start_h[:, None] + reach_h) * GW + start_w[:, None] + reach_w
    blank_slot = jax.random.randint(slot_key, (QUERY_TILES, 1), 0, SLOTS)
    slot_ids = jnp.arange(SLOTS)[None, :]
    source = jnp.clip(slot_ids - (slot_ids > blank_slot).astype(jnp.int32), 0, SLOTS - 2)
    picked = jnp.take_along_axis(window_tiles, source, axis=1)
    return jnp.where(slot_ids == blank_slot, -1, picked).astype(jnp.int32)


def draw_partner(key, part):
    key = jax.random.fold_in(key, 11)
    shuffled = jax.random.permutation(key, MEMBERS)
    partner_table = jnp.zeros((MEMBERS,), jnp.int32)
    partner_table = partner_table.at[shuffled[0::2]].set(shuffled[1::2])
    partner_table = partner_table.at[shuffled[1::2]].set(shuffled[0::2])
    return partner_table.astype(jnp.int32)


def block_scale(own_key, shape, shards, low, largest):
    def one(axis_at, shards_of):
        steps = jax.random.uniform(jax.random.fold_in(jax.random.fold_in(own_key, 6), axis_at), (shards_of,), jnp.float32, low / len(shards), largest / len(shards))
        return jnp.repeat(jnp.exp(steps), shape[axis_at] // shards_of).reshape((-1,) + (1,) * (len(shape) - axis_at - 1))

    loudness = one(*shards[0])
    for cut in shards[1:]:
        loudness = loudness * one(*cut)
    return loudness


def bell_draw(stream_key, shape, spread, reach, shards=(), kind=jnp.bfloat16):
    values = spread * jax.random.normal(stream_key, shape, jnp.float32)
    if shards:
        values = values * block_scale(stream_key, shape, shards, -0.22, 0.18)
    return jnp.clip(values, -reach, reach).astype(kind)


def setup_inputs(seed: int = 0) -> dict:
    splits = jax.random.split(jax.random.key(seed), 7)
    query_states = draw_query_states(jax.random.fold_in(splits[6], 71), 0)
    key_states = draw_key_states(jax.random.fold_in(splits[6], 71), 0)
    value_states = bell_draw(splits[2], (MEMBERS, TOKENS, HEADS * HEAD_DIM), 1.0, 6.0, ((0, 16), (1, 16)))
    tile_pattern = draw_tile_pattern(jax.random.fold_in(splits[6], 71), 0)
    strength = jnp.clip(jnp.exp(jax.random.uniform(splits[4], (MEMBERS,), jnp.float32, math.log(1.0), math.log(8.0))), 1.0, 8.0)
    partner = draw_partner(jax.random.fold_in(splits[6], 71), 0)
    return dict(query_states=query_states, key_states=key_states, value_states=value_states, tile_pattern=tile_pattern, strength=strength, partner=partner)


def head_reference(query_head, key_head, value_head, tile_index, is_valid):
    tile_size = TILE_T * TILE_H * TILE_W
    tile_count = GT * GH * GW
    score_scale = 1.0 / math.sqrt(HEAD_DIM)
    query_tiles = query_head.astype(jnp.float32).reshape(QUERY_TILES, tile_size, HEAD_DIM)
    key_tiles = jnp.take(key_head.astype(jnp.float32).reshape(tile_count, tile_size, HEAD_DIM), tile_index, axis=0)
    value_tiles = jnp.take(value_head.astype(jnp.float32).reshape(tile_count, tile_size, HEAD_DIM), tile_index, axis=0)
    scores = jnp.einsum('iqd,iskd->iqsk', query_tiles, key_tiles) * score_scale
    scores = jnp.where(is_valid[:, None, :, None], scores, -1e+30)
    maximum = lax.optimization_barrier(jnp.max(scores, axis=(2, 3), keepdims=True))
    exponent = jnp.exp(scores - maximum)
    totals = lax.optimization_barrier(jnp.sum(exponent, axis=(2, 3)))
    weights = lax.optimization_barrier(exponent.astype(jnp.bfloat16)).astype(jnp.float32)
    attended = jnp.einsum('iqsk,iskd->iqd', weights, value_tiles) / totals[:, :, None]
    return attended.astype(jnp.bfloat16).reshape(QUERY_TILES * tile_size, HEAD_DIM)

def by_heads(states):
    return states.reshape(states.shape[0], HEADS, HEAD_DIM).transpose(1, 0, 2)

def reference(query_states, key_states, value_states, tile_pattern, strength, partner):
    is_valid = tile_pattern >= 0
    tile_index = jnp.maximum(tile_pattern, 0).astype(jnp.int32)

    def one_head(triple_head):
        return head_reference(triple_head[0], triple_head[1], triple_head[2], tile_index, is_valid)

    def one_member(triple):
        outputs = lax.map(one_head, (by_heads(triple[0]), by_heads(triple[1]), by_heads(triple[2])))
        return outputs.transpose(1, 0, 2).reshape(QUERY_TOKENS, HEADS * HEAD_DIM)
    attended = lax.map(one_member, (query_states, key_states, value_states))
    stored = lax.optimization_barrier(attended).astype(jnp.float32)
    partner_rows = jnp.take(stored, partner.astype(jnp.int32), axis=0)
    strength_col = strength[:, None, None]
    return (partner_rows + strength_col * (stored - partner_rows)).astype(jnp.bfloat16)
```

```python
import functools
import math

import jax
import jax.numpy as jnp
from jax import lax
from jax.experimental import pallas as pl
from jax.experimental.pallas import tpu as pltpu
from jax.sharding import PartitionSpec as P

MESH = pl.DeviceIdType.MESH
HEAD = 128
TILE = 192
RING = 8
NEG = -1e30
BIG = 1e30
NT = (((1,), (1,)), ((), ()))


def kernel(
    pattern, strength, partner, q_hbm, k_hbm, v_hbm, out,
    kb, vb, qb, qbd, vt, scores, probs, valid, own, own_lse,
    stage, stage_lse, got, got_lse, att, comb, sel, gst,
    k_sem, v_sem, q_sem, ag_sem, rs_sem, lse_sem, comb_sem, out_sem,
    ks_send, vs_send, qs_send, ag_send, rs_send, lse_send, att_send, gst_send,
):
    seq = lax.axis_index("seq")
    cfg = lax.axis_index("cfg")
    x = lax.div(seq, RING)
    z = lax.rem(seq, RING)
    ox = 1 - x
    pairs = kb.shape[0]
    rows = kb.shape[1] // 2
    qrows = q_hbm.shape[1]
    width = 2 * HEAD
    half = pairs * width
    lanes = 2 * TILE
    members = comb.shape[1]
    factor = math.log2(math.e) / math.sqrt(HEAD)

    def ring(a):
        return lax.rem(a + 2 * RING, RING)

    def remote(src, dst, send, recv, to_seq, to_cfg):
        return pltpu.make_async_remote_copy(
            src_ref=src, dst_ref=dst, send_sem=send, recv_sem=recv,
            device_id={"seq": to_seq, "cfg": to_cfg}, device_id_type=MESH,
        )

    def wait(ref, sem):
        pltpu.make_async_copy(ref, ref, sem).wait()

    barrier = pltpu.get_barrier_semaphore()

    def greet(to_seq, to_cfg):
        pl.semaphore_signal(
            barrier, inc=1, device_id={"seq": to_seq, "cfg": to_cfg}, device_id_type=MESH
        )

    greet(x * RING + ring(z + 1), cfg)
    greet(x * RING + ring(z - 1), cfg)
    for step in range(1, members):
        greet(seq, lax.rem(cfg + step, members))
    for step in range(members):
        greet(ox * RING + z, lax.rem(cfg + step, members))

    def local(p):
        cols = pl.ds(pl.multiple_of(x * half + p * width, width), width)
        mine = pl.ds(pl.multiple_of(x * rows, 64), rows)
        pltpu.make_async_copy(k_hbm.at[0, :, cols], kb.at[p, mine], k_sem.at[p]).start()
        pltpu.make_async_copy(v_hbm.at[0, :, cols], vb.at[p, mine], v_sem.at[p]).start()

    def local_q(p):
        cols = pl.ds(pl.multiple_of(x * half + p * width, width), width)
        mine = pl.ds(pl.multiple_of(x * qrows, 32), qrows)
        pltpu.make_async_copy(q_hbm.at[0, :, cols], qb.at[p, z, mine], q_sem.at[p]).start()

    def swap_kv(p):
        cols = pl.ds(pl.multiple_of(ox * half + p * width, width), width)
        mine = pl.ds(pl.multiple_of(x * rows, 64), rows)
        to = ox * RING + z
        remote(k_hbm.at[0, :, cols], kb.at[p, mine], ks_send, k_sem.at[p], to, cfg).start()
        remote(v_hbm.at[0, :, cols], vb.at[p, mine], vs_send, v_sem.at[p], to, cfg).start()

    def swap_q(p):
        cols = pl.ds(pl.multiple_of(ox * half + p * width, width), width)
        mine = pl.ds(pl.multiple_of(x * qrows, 32), qrows)
        to = ox * RING + z
        remote(q_hbm.at[0, :, cols], qb.at[p, z, mine], qs_send, q_sem.at[p], to, cfg).start()

    for p in range(pairs):
        local_q(p)
    for p in range(pairs):
        local(p)

    for s in range(6):
        tile = 3 * z + (s % 3) + (0 if s < 3 else 3 * RING)
        hit = jnp.max((pattern[...] == tile).astype(jnp.float32), axis=1, keepdims=True)
        lane = lax.broadcasted_iota(jnp.int32, (1, lanes), 1)
        first = lax.rem(lane, TILE) < qrows
        for b in range(RING):
            valid[b, s : s + 1, :] = jnp.where(
                first, hit[b // 2 : b // 2 + 1, :], hit[4 + b // 2 : 5 + b // 2, :]
            )

    qbd[...] = jnp.zeros_like(qbd)
    vt[width : width + 16, :] = jnp.ones((16, vt.shape[1]), vt.dtype)

    pl.semaphore_wait(barrier, 2 + (members - 1) + members)

    swap_q(0)
    swap_q(1)
    swap_kv(0)
    swap_q(2)
    swap_q(3)
    swap_kv(1)
    swap_q(4)
    swap_kv(2)

    def sign(p):
        return 1 - 2 * lax.rem(p, 2)

    def gather_send(p, step):
        sg = sign(p)
        block = qb.at[p, ring(z - sg * step)]
        remote(block, block, ag_send, ag_sem.at[p, step], x * RING + ring(z + sg), cfg).start()
        if step < 3:
            block = qb.at[p, ring(z + sg * step)]
            remote(
                block, block, ag_send, ag_sem.at[p, 4 + step], x * RING + ring(z - sg), cfg
            ).start()

    def gather_wait(p, step):
        sg = sign(p)
        wait(qb.at[p, ring(z - sg * (step + 1))], ag_sem.at[p, step])
        if step < 3:
            wait(qb.at[p, ring(z + sg * (step + 1))], ag_sem.at[p, 4 + step])

    def turn_values(p):
        vt[0:width, :] = vb[p].T

    def compute(p, j):
        sg = -sign(p)
        b0 = ring(z + sg * (4 - j))
        b1 = ring(z - sg * (3 - j))
        for n, b in enumerate((b0, b1)):
            qbd[n * lanes : n * lanes + TILE, 0:HEAD] = qb[p, b, :, 0:HEAD]
            qbd[n * lanes + TILE : (n + 1) * lanes, HEAD:width] = qb[p, b, :, HEAD:width]
        top = jnp.full((1, 2 * lanes), NEG, jnp.float32)
        for s in range(6):
            part = lax.dot_general(
                kb[p, s * TILE : (s + 1) * TILE, :], qbd[...], NT,
                preferred_element_type=jnp.float32,
            )
            scores[s * TILE : (s + 1) * TILE, :] = part
            here = jnp.max(part, axis=0, keepdims=True)
            ok = jnp.concatenate([valid[b0, s : s + 1, :], valid[b1, s : s + 1, :]], axis=1)
            top = jnp.maximum(top, jnp.where(ok > 0.0, here, NEG))
        for s in range(6):
            ok = jnp.concatenate([valid[b0, s : s + 1, :], valid[b1, s : s + 1, :]], axis=1)
            shift = jnp.where(ok > 0.0, top, BIG)
            probs[s * TILE : (s + 1) * TILE, :] = jnp.exp2(
                (scores[s * TILE : (s + 1) * TILE, :] - shift) * factor
            ).astype(jnp.bfloat16)
        both = jnp.dot(vt[...], probs[...], preferred_element_type=jnp.float32)
        total = both[width : width + 1, :]
        some = total > 0.0
        safe = jnp.where(some, total, 1.0)
        lse = jnp.where(some, top * factor + jnp.log2(safe), NEG)
        scale = jnp.where(some, 1.0 / safe, 0.0)
        lane = lax.broadcasted_iota(jnp.int32, (1, 2 * lanes), 1)
        first = lax.rem(lane, lanes) < TILE
        o = jnp.where(first, both[0:HEAD, :], both[HEAD:width, :]) * scale
        slot = lax.rem(p, 3)
        for n in range(2):
            own[slot, 2 * j + n] = o[:, n * lanes : (n + 1) * lanes]
            own_lse[slot, 2 * j + n] = lse[:, n * lanes : (n + 1) * lanes]

    def merge(oa, la, ob, lb):
        m = jnp.maximum(la, lb)
        wa = jnp.exp2(la - m)
        wb = jnp.exp2(lb - m)
        t = wa + wb
        r = 1.0 / t
        return oa * (wa * r) + ob * (wb * r), m + jnp.log2(t)

    def reduce_send(p, step):
        sg = -sign(p)
        slot = lax.rem(p, 3)
        chains = ((0, step, 2 * step, z + sg),)
        if step < 3:
            chains += ((1, 4 + step, 2 * step + 1, z - sg),)
        for _, at, mine, to in chains:
            o = own[slot, mine]
            lse = own_lse[slot, mine]
            if step > 0:
                wait(got.at[p, at - 1], rs_sem.at[p, at - 1])
                wait(got_lse.at[p, at - 1], lse_sem.at[p, at - 1])
                o, lse = merge(
                    o, lse, got[p, at - 1].astype(jnp.float32), got_lse[p, at - 1]
                )
            stage[p, at] = o.astype(jnp.bfloat16)
            stage_lse[p, at] = lse
            there = x * RING + ring(to)
            remote(stage.at[p, at], got.at[p, at], rs_send, rs_sem.at[p, at], there, cfg).start()
            remote(
                stage_lse.at[p, at], got_lse.at[p, at], lse_send, lse_sem.at[p, at], there, cfg
            ).start()

    def finish(p):
        slot = lax.rem(p, 3)
        o = own[slot, 7]
        lse = own_lse[slot, 7]
        for at in (6, 3):
            wait(got.at[p, at], rs_sem.at[p, at])
            wait(got_lse.at[p, at], lse_sem.at[p, at])
            o, lse = merge(o, lse, got[p, at].astype(jnp.float32), got_lse[p, at])
        turned = o.T.astype(jnp.bfloat16)
        g = lax.div(p, 2)
        e = lax.rem(p, 2)
        for c in range(8):
            att[g, e * 8 + c] = turned[c * 48 : (c + 1) * 48, :]

    def spread(g):
        pltpu.make_async_copy(att.at[g, cfg], comb.at[g, cfg], comb_sem.at[g]).start()
        for step in range(1, members):
            c = lax.rem(cfg + step, members)
            remote(att.at[g, c], comb.at[g, cfg], att_send, comb_sem.at[g], seq, c).start()

    def combine(g):
        wait(comb.at[g], comb_sem.at[g])
        sel[...] = comb[g]
        hh = lax.div(cfg, 4)
        tx = lax.rem(lax.div(cfg, 2), 2)
        start = pl.multiple_of(lax.rem(cfg, 2) * 48, 16)
        cols = pl.ds(pl.multiple_of(x * half + g * 2 * width + hh * HEAD, HEAD), HEAD)
        for m in range(members):
            a = sel[m].astype(jnp.float32)
            other = sel[partner[m]].astype(jnp.float32)
            gst[g, m] = (other + strength[m] * (a - other)).astype(jnp.bfloat16)
        for step in range(members):
            m = lax.rem(cfg + step, members)
            there = remote(
                gst.at[g, m], out.at[0, pl.ds(start, 48), cols], gst_send, out_sem,
                tx * RING + z, m,
            )
            if step == 0:
                here = pltpu.make_async_copy(
                    gst.at[g, m], out.at[0, pl.ds(start, 48), cols], out_sem
                )

                @pl.when(tx == x)
                def _():
                    here.start()

                @pl.when(tx != x)
                def _():
                    there.start()

            else:
                there.start()

    def body(t, carry):
        i = t - 2
        ahead2 = (i + 2 < pairs)
        ahead1 = (i + 1 >= 0) & (i + 1 < pairs)
        now = (i >= 0) & (i < pairs)
        behind1 = (i >= 1) & (i < pairs + 1)
        behind2 = (i >= 2) & (i < pairs + 2)

        @pl.when(ahead2)
        def _():
            wait(qb.at[i + 2, z], q_sem.at[i + 2])
            gather_send(i + 2, 0)

        @pl.when(ahead1)
        def _():
            gather_wait(i + 1, 1)
            gather_send(i + 1, 2)

        @pl.when(now)
        def _():
            gather_wait(i, 3)
            wait(kb.at[i], k_sem.at[i])
            wait(vb.at[i], v_sem.at[i])

            @pl.when(i + 3 < pairs)
            def _():
                swap_kv(i + 3)

            @pl.when(i + 5 < pairs)
            def _():
                swap_q(i + 5)

            turn_values(i)
            lax.fori_loop(0, 2, lambda j, c: (compute(i, j), c)[1], 0)
            reduce_send(i, 0)

        @pl.when(behind1)
        def _():
            reduce_send(i - 1, 2)

        @pl.when(behind2)
        def _():
            finish(i - 2)

            @pl.when(lax.rem(i, 2) == 1)
            def _():
                spread(lax.div(i - 3, 2))

        @pl.when(ahead2)
        def _():
            gather_wait(i + 2, 0)
            gather_send(i + 2, 1)

        @pl.when(ahead1)
        def _():
            gather_wait(i + 1, 2)
            gather_send(i + 1, 3)

        @pl.when(now)
        def _():
            lax.fori_loop(2, 4, lambda j, c: (compute(i, j), c)[1], 0)
            reduce_send(i, 1)

        @pl.when(behind1)
        def _():
            reduce_send(i - 1, 3)

        @pl.when((i >= 4) & (lax.rem(i + 2, 2) == 0))
        def _():
            combine(lax.div(i - 4, 2))

        return carry

    lax.fori_loop(0, pairs + 5, body, 0)

    wait(out.at[0], out_sem)
    wait(kb.at[:, 0:rows], ks_send)
    wait(vb.at[:, 0:rows], vs_send)
    wait(qb.at[:, 0, 0:qrows], qs_send)
    wait(qb.at[:, 0:7], ag_send)
    wait(stage, rs_send)
    wait(stage_lse, lse_send)
    wait(att.at[:, 0 : members - 1], att_send)
    tx = lax.rem(lax.div(cfg, 2), 2)

    @pl.when(tx == x)
    def _():
        wait(gst.at[:, 0 : members - 1], gst_send)

    @pl.when(tx != x)
    def _():
        wait(gst, gst_send)


def body(query_states, key_states, value_states, tile_pattern, strength, partner):
    rows = key_states.shape[1]
    qrows = query_states.shape[1]
    pairs = query_states.shape[2] // (4 * HEAD)
    members = lax.axis_size("cfg")
    width, lanes = 2 * HEAD, 2 * TILE
    bf, f32 = jnp.bfloat16, jnp.float32
    vm = pltpu.VMEM
    dma = pltpu.SemaphoreType.DMA
    return pl.pallas_call(
        kernel,
        out_shape=jax.ShapeDtypeStruct(query_states.shape, bf),
        in_specs=[
            pl.BlockSpec(memory_space=pltpu.VMEM),
            pl.BlockSpec(memory_space=pltpu.SMEM),
            pl.BlockSpec(memory_space=pltpu.SMEM),
            pl.BlockSpec(memory_space=pl.ANY),
            pl.BlockSpec(memory_space=pl.ANY),
            pl.BlockSpec(memory_space=pl.ANY),
        ],
        out_specs=pl.BlockSpec(memory_space=pl.ANY),
        scratch_shapes=[
            vm((pairs, 2 * rows, width), bf),
            vm((pairs, 2 * rows, width), bf),
            vm((pairs, RING, 2 * qrows, width), bf),
            vm((2 * lanes, width), bf),
            vm((width + 16, 2 * rows), bf),
            vm((2 * rows, 2 * lanes), f32),
            vm((2 * rows, 2 * lanes), bf),
            vm((RING, 8, lanes), f32),
            vm((3, 8, HEAD, lanes), f32),
            vm((3, 8, 1, lanes), f32),
            vm((pairs, 7, HEAD, lanes), bf),
            vm((pairs, 7, 1, lanes), f32),
            vm((pairs, 7, HEAD, lanes), bf),
            vm((pairs, 7, 1, lanes), f32),
            vm((pairs // 2, members, 48, HEAD), bf),
            vm((pairs // 2, members, 48, HEAD), bf),
            vm((members, 48, HEAD), bf),
            vm((pairs // 2, members, 48, HEAD), bf),
            dma((pairs,)),
            dma((pairs,)),
            dma((pairs,)),
            dma((pairs, 7)),
            dma((pairs, 7)),
            dma((pairs, 7)),
            dma((pairs // 2,)),
            dma,
            dma,
            dma,
            dma,
            dma,
            dma,
            dma,
            dma,
            dma,
        ],
        compiler_params=pltpu.CompilerParams(
            collective_id=0, has_side_effects=True, vmem_limit_bytes=60 * 1024 * 1024
        ),
        cost_estimate=pl.CostEstimate(
            flops=30_000_000_000, bytes_accessed=24_000_000, transcendentals=28_000_000
        ),
    )(tile_pattern, strength, partner, query_states, key_states, value_states)


def solution(mesh):
    return jax.shard_map(
        body,
        mesh=mesh,
        in_specs=(
            P("cfg", "seq", None),
            P("cfg", "seq", None),
            P("cfg", "seq", None),
            P(),
            P(),
            P(),
        ),
        out_specs=P("cfg", "seq", None),
        check_vma=False,
    )
```

```python
import functools
import math

import jax
import jax.numpy as jnp
from jax import lax
from jax.experimental import pallas as pl
from jax.experimental.pallas import tpu as pltpu
from jax.sharding import PartitionSpec as P

MESH = pl.DeviceIdType.MESH
HEAD = 128
TILE = 192
RING = 8
NEG = -1e30
BIG = 1e30
DEPTH = 2
LEAD = 12
NT = (((1,), (1,)), ((), ()))


def kernel(
    pattern, strength, partner, q_hbm, k_hbm, v_hbm, out,
    kb, vb, qb, qbd, vt, scores, probs, valid, own, own_lse,
    stage, stage_lse, got, got_lse, att, comb, sel, gst,
    k_sem, v_sem, q_sem, ag_sem, rs_sem, lse_sem, comb_sem, out_sem,
    ks_send, vs_send, qs_send, ag_send, rs_send, lse_send, att_send, gst_send,
):
    seq = lax.axis_index("seq")
    cfg = lax.axis_index("cfg")
    x = lax.div(seq, RING)
    z = lax.rem(seq, RING)
    ox = 1 - x
    hi = lax.rem(lax.div(cfg, 2), 2)
    hx = lax.rem(x + hi, 2)
    pairs = kb.shape[0]
    rows = kb.shape[1] // 2
    qrows = q_hbm.shape[1]
    width = 2 * HEAD
    half = pairs * width
    lanes = 2 * TILE
    members = comb.shape[1]
    factor = math.log2(math.e) / math.sqrt(HEAD)

    def ring(a):
        return lax.rem(a + 2 * RING, RING)

    def remote(src, dst, send, recv, to_seq, to_cfg):
        return pltpu.make_async_remote_copy(
            src_ref=src, dst_ref=dst, send_sem=send, recv_sem=recv,
            device_id={"seq": to_seq, "cfg": to_cfg}, device_id_type=MESH,
        )

    def wait(ref, sem):
        pltpu.make_async_copy(ref, ref, sem).wait()

    barrier = pltpu.get_barrier_semaphore()

    def greet(to_seq, to_cfg):
        pl.semaphore_signal(
            barrier, inc=1, device_id={"seq": to_seq, "cfg": to_cfg}, device_id_type=MESH
        )

    greet(x * RING + ring(z + 1), cfg)
    greet(x * RING + ring(z - 1), cfg)
    for step in range(1, members):
        c = lax.rem(cfg + step, members)

        @pl.when(lax.rem(lax.div(c, 2), 2) == hi)
        def _():
            greet(seq, c)

    for step in range(members):
        greet(ox * RING + z, lax.rem(cfg + step, members))

    def local(p):
        cols = pl.ds(pl.multiple_of(hx * half + p * width, width), width)
        mine = pl.ds(pl.multiple_of(x * rows, 64), rows)
        pltpu.make_async_copy(k_hbm.at[0, :, cols], kb.at[p, mine], k_sem.at[p]).start()
        pltpu.make_async_copy(v_hbm.at[0, :, cols], vb.at[p, mine], v_sem.at[p]).start()

    def local_q(p):
        cols = pl.ds(pl.multiple_of(hx * half + p * width, width), width)
        mine = pl.ds(pl.multiple_of(x * qrows, 32), qrows)
        pltpu.make_async_copy(q_hbm.at[0, :, cols], qb.at[p, z, mine], q_sem.at[p]).start()

    def swap_kv(p):
        cols = pl.ds(pl.multiple_of((1 - hx) * half + p * width, width), width)
        mine = pl.ds(pl.multiple_of(x * rows, 64), rows)
        to = ox * RING + z
        remote(k_hbm.at[0, :, cols], kb.at[p, mine], ks_send, k_sem.at[p], to, cfg).start()
        remote(v_hbm.at[0, :, cols], vb.at[p, mine], vs_send, v_sem.at[p], to, cfg).start()

    def swap_q(p):
        cols = pl.ds(pl.multiple_of((1 - hx) * half + p * width, width), width)
        mine = pl.ds(pl.multiple_of(x * qrows, 32), qrows)
        to = ox * RING + z
        remote(q_hbm.at[0, :, cols], qb.at[p, z, mine], qs_send, q_sem.at[p], to, cfg).start()

    for p in range(pairs):
        local_q(p)
    for p in range(pairs):
        local(p)

    for s in range(6):
        tile = 3 * z + (s % 3) + (0 if s < 3 else 3 * RING)
        hit = jnp.max((pattern[...] == tile).astype(jnp.float32), axis=1, keepdims=True)
        lane = lax.broadcasted_iota(jnp.int32, (1, lanes), 1)
        first = lax.rem(lane, TILE) < qrows
        for b in range(RING):
            valid[b, s : s + 1, :] = jnp.where(
                first, hit[b // 2 : b // 2 + 1, :], hit[4 + b // 2 : 5 + b // 2, :]
            )

    qbd[...] = jnp.zeros_like(qbd)
    vt[width : width + 16, :] = jnp.ones((16, vt.shape[1]), vt.dtype)

    pl.semaphore_wait(barrier, 2 + (members // 2 - 1) + members)

    swap_q(0)
    swap_q(1)
    swap_q(2)
    swap_kv(0)

    def sign(p):
        return 1 - 2 * lax.rem(p, 2)

    def gather_send(p, step):
        sg = sign(p)
        block = qb.at[p, ring(z - sg * step)]
        remote(block, block, ag_send, ag_sem.at[p, step], x * RING + ring(z + sg), cfg).start()

        @pl.when(step < 3)
        def _():
            block = qb.at[p, ring(z + sg * step)]
            remote(
                block, block, ag_send, ag_sem.at[p, 4 + step], x * RING + ring(z - sg), cfg
            ).start()

    def gather_wait(p, step):
        sg = sign(p)
        wait(qb.at[p, ring(z - sg * (step + 1))], ag_sem.at[p, step])

        @pl.when(step < 3)
        def _():
            wait(qb.at[p, ring(z + sg * (step + 1))], ag_sem.at[p, 4 + step])

    def turn_values(p):
        vt[0:width, :] = vb[p].T

    def compute(p, j):
        sg = -sign(p)
        b0 = ring(z + sg * (4 - j))
        b1 = ring(z - sg * (3 - j))
        for n, b in enumerate((b0, b1)):
            qbd[n * lanes : n * lanes + TILE, 0:HEAD] = qb[p, b, :, 0:HEAD]
            qbd[n * lanes + TILE : (n + 1) * lanes, HEAD:width] = qb[p, b, :, HEAD:width]
        top = jnp.full((1, 2 * lanes), NEG, jnp.float32)
        for s in range(6):
            part = lax.dot_general(
                kb[p, s * TILE : (s + 1) * TILE, :], qbd[...], NT,
                preferred_element_type=jnp.float32,
            )
            scores[s * TILE : (s + 1) * TILE, :] = part
            here = jnp.max(part, axis=0, keepdims=True)
            ok = jnp.concatenate([valid[b0, s : s + 1, :], valid[b1, s : s + 1, :]], axis=1)
            top = jnp.maximum(top, jnp.where(ok > 0.0, here, NEG))
        for s in range(6):
            ok = jnp.concatenate([valid[b0, s : s + 1, :], valid[b1, s : s + 1, :]], axis=1)
            shift = jnp.where(ok > 0.0, top, BIG)
            probs[s * TILE : (s + 1) * TILE, :] = jnp.exp2(
                (scores[s * TILE : (s + 1) * TILE, :] - shift) * factor
            ).astype(jnp.bfloat16)
        both = jnp.dot(vt[...], probs[...], preferred_element_type=jnp.float32)
        total = both[width : width + 1, :]
        some = total > 0.0
        safe = jnp.where(some, total, 1.0)
        lse = jnp.where(some, top * factor + jnp.log2(safe), NEG)
        scale = jnp.where(some, 1.0 / safe, 0.0)
        lane = lax.broadcasted_iota(jnp.int32, (1, 2 * lanes), 1)
        first = lax.rem(lane, lanes) < TILE
        o = jnp.where(first, both[0:HEAD, :], both[HEAD:width, :]) * scale
        slot = lax.rem(p, 3)
        for n in range(2):
            own[slot, 2 * j + n] = o[:, n * lanes : (n + 1) * lanes]
            own_lse[slot, 2 * j + n] = lse[:, n * lanes : (n + 1) * lanes]

    def merge(oa, la, ob, lb):
        m = jnp.maximum(la, lb)
        wa = jnp.exp2(la - m)
        wb = jnp.exp2(lb - m)
        t = wa + wb
        r = 1.0 / t
        return oa * (wa * r) + ob * (wb * r), m + jnp.log2(t)

    def chain_send(p, at, o, lse, to):
        stage[p, at] = o.astype(jnp.bfloat16)
        stage_lse[p, at] = lse
        there = x * RING + ring(to)
        remote(stage.at[p, at], got.at[p, at], rs_send, rs_sem.at[p, at], there, cfg).start()
        remote(
            stage_lse.at[p, at], got_lse.at[p, at], lse_send, lse_sem.at[p, at], there, cfg
        ).start()

    def chain_merge(p, at, mine):
        slot = lax.rem(p, 3)
        wait(got.at[p, at], rs_sem.at[p, at])
        wait(got_lse.at[p, at], lse_sem.at[p, at])
        return merge(
            own[slot, mine], own_lse[slot, mine], got[p, at].astype(jnp.float32), got_lse[p, at]
        )

    def reduce_send(p, step):
        sg = -sign(p)
        slot = lax.rem(p, 3)

        @pl.when(step == 0)
        def _():
            chain_send(p, 0, own[slot, 0], own_lse[slot, 0], z + sg)
            chain_send(p, 4, own[slot, 1], own_lse[slot, 1], z - sg)

        @pl.when(step > 0)
        def _():
            o, lse = chain_merge(p, step - 1, 2 * step)
            chain_send(p, step, o, lse, z + sg)

        @pl.when((step > 0) & (step < 3))
        def _():
            o, lse = chain_merge(p, 3 + step, 2 * step + 1)
            chain_send(p, 4 + step, o, lse, z - sg)

    def finish(p):
        slot = lax.rem(p, 3)
        o = own[slot, 7]
        lse = own_lse[slot, 7]
        for at in (6, 3):
            wait(got.at[p, at], rs_sem.at[p, at])
            wait(got_lse.at[p, at], lse_sem.at[p, at])
            o, lse = merge(o, lse, got[p, at].astype(jnp.float32), got_lse[p, at])
        turned = o.T.astype(jnp.bfloat16)
        g = lax.div(p, 2)
        e = lax.rem(p, 2)
        for c in range(8):
            att[g, e * 8 + c] = turned[c * 48 : (c + 1) * 48, :]

    def share(c):
        lo = lax.rem(hx + lax.rem(lax.div(c, 2), 2), 2)
        return lo, lax.div(c, 4) * 4 + (1 - lo) * 2 + lax.rem(c, 2)

    def spread(g):
        _, mine = share(cfg)
        pltpu.make_async_copy(att.at[g, mine], comb.at[g, cfg], comb_sem.at[g]).start()
        for step in range(1, members):
            c = lax.rem(cfg + step, members)
            lo, which = share(c)
            remote(
                att.at[g, which], comb.at[g, cfg], att_send, comb_sem.at[g], lo * RING + z, c
            ).start()

    def combine(g):
        wait(comb.at[g], comb_sem.at[g])
        sel[...] = comb[g]
        hh = lax.div(cfg, 4)
        start = pl.multiple_of(lax.rem(cfg, 2) * 48, 16)
        cols = pl.ds(pl.multiple_of(hx * half + g * 2 * width + hh * HEAD, HEAD), HEAD)
        for m in range(members):
            a = sel[m].astype(jnp.float32)
            other = sel[partner[m]].astype(jnp.float32)
            gst[g, m] = (other + strength[m] * (a - other)).astype(jnp.bfloat16)
        for step in range(members):
            m = lax.rem(cfg + step, members)
            remote(
                gst.at[g, m], out.at[0, pl.ds(start, 48), cols], gst_send, out_sem,
                ox * RING + z, m,
            ).start()

    def body(u, carry):
        t = u - LEAD
        i = lax.div(t + 16, 4) - 4
        j = lax.rem(t + 16, 4)
        hop = lax.rem(4 - j, 4)
        back = lax.div(t - 3 * hop + 32, 4) - 8
        ahead = back + 3
        now = (i >= 0) & (i < pairs)

        @pl.when((ahead >= 0) & (ahead < pairs))
        def _():
            @pl.when(hop == 0)
            def _():
                wait(qb.at[ahead, z], q_sem.at[ahead])

            @pl.when(hop > 0)
            def _():
                gather_wait(ahead, hop - 1)

            gather_send(ahead, hop)

        @pl.when(j == 0)
        def _():
            @pl.when((i >= -2) & (i + 5 < pairs))
            def _():
                swap_q(i + 5)

            @pl.when(now)
            def _():
                wait(kb.at[i], k_sem.at[i])
                wait(vb.at[i], v_sem.at[i])

            @pl.when((i >= 1 - DEPTH) & (i + DEPTH < pairs))
            def _():
                swap_kv(i + DEPTH)

            @pl.when(now)
            def _():
                gather_wait(i, 3)
                turn_values(i)

        @pl.when(now)
        def _():
            compute(i, j)

        @pl.when((back >= 0) & (back < pairs))
        def _():
            reduce_send(back, hop)

        @pl.when((j == 0) & (i >= 3) & (i - 3 < pairs))
        def _():
            finish(i - 3)

            @pl.when(lax.rem(i, 2) == 0)
            def _():
                spread(lax.div(i - 4, 2))

        @pl.when((t >= 19) & (lax.rem(t + 32 - 19, 8) == 0))
        def _():
            combine(lax.div(t - 19, 8))

        return carry

    lax.fori_loop(0, LEAD + 4 * (pairs - 1) + 16, body, 0)

    wait(out.at[0], out_sem)
    wait(kb.at[:, 0:rows], ks_send)
    wait(vb.at[:, 0:rows], vs_send)
    wait(qb.at[:, 0, 0:qrows], qs_send)
    wait(qb.at[:, 0:7], ag_send)
    wait(stage, rs_send)
    wait(stage_lse, lse_send)
    wait(att.at[:, 0 : members - 1], att_send)
    wait(gst, gst_send)


def body(query_states, key_states, value_states, tile_pattern, strength, partner):
    rows = key_states.shape[1]
    qrows = query_states.shape[1]
    pairs = query_states.shape[2] // (4 * HEAD)
    members = lax.axis_size("cfg")
    width, lanes = 2 * HEAD, 2 * TILE
    bf, f32 = jnp.bfloat16, jnp.float32
    vm = pltpu.VMEM
    dma = pltpu.SemaphoreType.DMA
    return pl.pallas_call(
        kernel,
        out_shape=jax.ShapeDtypeStruct(query_states.shape, bf),
        in_specs=[
            pl.BlockSpec(memory_space=pltpu.VMEM),
            pl.BlockSpec(memory_space=pltpu.SMEM),
            pl.BlockSpec(memory_space=pltpu.SMEM),
            pl.BlockSpec(memory_space=pl.ANY),
            pl.BlockSpec(memory_space=pl.ANY),
            pl.BlockSpec(memory_space=pl.ANY),
        ],
        out_specs=pl.BlockSpec(memory_space=pl.ANY),
        scratch_shapes=[
            vm((pairs, 2 * rows, width), bf),
            vm((pairs, 2 * rows, width), bf),
            vm((pairs, RING, 2 * qrows, width), bf),
            vm((2 * lanes, width), bf),
            vm((width + 16, 2 * rows), bf),
            vm((2 * rows, 2 * lanes), f32),
            vm((2 * rows, 2 * lanes), bf),
            vm((RING, 8, lanes), f32),
            vm((3, 8, HEAD, lanes), f32),
            vm((3, 8, 1, lanes), f32),
            vm((pairs, 7, HEAD, lanes), bf),
            vm((pairs, 7, 1, lanes), f32),
            vm((pairs, 7, HEAD, lanes), bf),
            vm((pairs, 7, 1, lanes), f32),
            vm((pairs // 2, members, 48, HEAD), bf),
            vm((pairs // 2, members, 48, HEAD), bf),
            vm((members, 48, HEAD), bf),
            vm((pairs // 2, members, 48, HEAD), bf),
            dma((pairs,)),
            dma((pairs,)),
            dma((pairs,)),
            dma((pairs, 7)),
            dma((pairs, 7)),
            dma((pairs, 7)),
            dma((pairs // 2,)),
            dma,
            dma,
            dma,
            dma,
            dma,
            dma,
            dma,
            dma,
            dma,
        ],
        compiler_params=pltpu.CompilerParams(
            collective_id=0, has_side_effects=True, vmem_limit_bytes=60 * 1024 * 1024
        ),
        cost_estimate=pl.CostEstimate(
            flops=30_000_000_000, bytes_accessed=24_000_000, transcendentals=28_000_000
        ),
    )(tile_pattern, strength, partner, query_states, key_states, value_states)


def solution(mesh):
    return jax.shard_map(
        body,
        mesh=mesh,
        in_specs=(
            P("cfg", "seq", None),
            P("cfg", "seq", None),
            P("cfg", "seq", None),
            P(),
            P(),
            P(),
        ),
        out_specs=P("cfg", "seq", None),
        check_vma=False,
    )
```

```python
import functools
import math

import jax
import jax.numpy as jnp
from jax import lax
from jax.experimental import pallas as pl
from jax.experimental.pallas import tpu as pltpu
from jax.sharding import PartitionSpec as P

MESH = pl.DeviceIdType.MESH
HEAD = 128
TILE = 192
RING = 8
NEG = -1e30
BIG = 1e30
DEPTH = 2
LEAD = 12
NT = (((1,), (1,)), ((), ()))


def kernel(
    pattern, strength, partner, q_hbm, k_hbm, v_hbm, out,
    kb, vb, qb, qbd, vt, scores, probs, valid, own, own_lse,
    stage, stage_lse, got, got_lse, att, comb, sel, gst,
    k_sem, v_sem, q_sem, ag_sem, rs_sem, lse_sem, comb_sem, out_sem,
    ks_send, vs_send, qs_send, ag_send, rs_send, lse_send, att_send, gst_send,
):
    seq = lax.axis_index("seq")
    cfg = lax.axis_index("cfg")
    x = lax.div(seq, RING)
    z = lax.rem(seq, RING)
    ox = 1 - x
    hi = lax.rem(lax.div(cfg, 2), 2)
    hx = lax.rem(x + hi, 2)
    pairs = kb.shape[0]
    rows = kb.shape[1] // 2
    qrows = q_hbm.shape[1]
    width = 2 * HEAD
    half = pairs * width
    lanes = 2 * TILE
    members = comb.shape[1]
    factor = math.log2(math.e) / math.sqrt(HEAD)

    def ring(a):
        return lax.rem(a + 2 * RING, RING)

    def remote(src, dst, send, recv, to_seq, to_cfg):
        return pltpu.make_async_remote_copy(
            src_ref=src, dst_ref=dst, send_sem=send, recv_sem=recv,
            device_id={"seq": to_seq, "cfg": to_cfg}, device_id_type=MESH,
        )

    def wait(ref, sem):
        pltpu.make_async_copy(ref, ref, sem).wait()

    barrier = pltpu.get_barrier_semaphore()

    def greet(to_seq, to_cfg):
        pl.semaphore_signal(
            barrier, inc=1, device_id={"seq": to_seq, "cfg": to_cfg}, device_id_type=MESH
        )

    greet(x * RING + ring(z + 1), cfg)
    greet(x * RING + ring(z - 1), cfg)
    for step in range(1, members):
        c = lax.rem(cfg + step, members)

        @pl.when(lax.rem(lax.div(c, 2), 2) == hi)
        def _():
            greet(seq, c)

    for step in range(members):
        greet(ox * RING + z, lax.rem(cfg + step, members))

    def local(p):
        cols = pl.ds(pl.multiple_of(hx * half + p * width, width), width)
        mine = pl.ds(pl.multiple_of(x * rows, 64), rows)
        pltpu.make_async_copy(k_hbm.at[0, :, cols], kb.at[p, mine], k_sem.at[p]).start()
        pltpu.make_async_copy(v_hbm.at[0, :, cols], vb.at[p, mine], v_sem.at[p]).start()

    def local_q(p):
        cols = pl.ds(pl.multiple_of(hx * half + p * width, width), width)
        mine = pl.ds(pl.multiple_of(x * qrows, 32), qrows)
        pltpu.make_async_copy(q_hbm.at[0, :, cols], qb.at[p, z, mine], q_sem.at[p]).start()

    def swap_kv(p):
        cols = pl.ds(pl.multiple_of((1 - hx) * half + p * width, width), width)
        mine = pl.ds(pl.multiple_of(x * rows, 64), rows)
        to = ox * RING + z
        remote(k_hbm.at[0, :, cols], kb.at[p, mine], ks_send, k_sem.at[p], to, cfg).start()
        remote(v_hbm.at[0, :, cols], vb.at[p, mine], vs_send, v_sem.at[p], to, cfg).start()

    def swap_q(p):
        cols = pl.ds(pl.multiple_of((1 - hx) * half + p * width, width), width)
        mine = pl.ds(pl.multiple_of(x * qrows, 32), qrows)
        to = ox * RING + z
        remote(q_hbm.at[0, :, cols], qb.at[p, z, mine], qs_send, q_sem.at[p], to, cfg).start()

    for p in range(pairs):
        local_q(p)
    for p in range(pairs):
        local(p)

    for s in range(6):
        tile = 3 * z + (s % 3) + (0 if s < 3 else 3 * RING)
        hit = jnp.max((pattern[...] == tile).astype(jnp.float32), axis=1, keepdims=True)
        lane = lax.broadcasted_iota(jnp.int32, (1, lanes), 1)
        first = lax.rem(lane, TILE) < qrows
        for b in range(RING):
            valid[b, s : s + 1, :] = jnp.where(
                first, hit[b // 2 : b // 2 + 1, :], hit[4 + b // 2 : 5 + b // 2, :]
            )

    qbd[...] = jnp.zeros_like(qbd)
    vt[width : width + 16, :] = jnp.ones((16, vt.shape[1]), vt.dtype)

    pl.semaphore_wait(barrier, 2 + (members // 2 - 1) + members)

    for p in range(pairs):
        swap_q(p)
    swap_kv(0)

    def sign(p):
        return 1 - 2 * lax.rem(p, 2)

    def gather_send(p, step):
        sg = sign(p)
        block = qb.at[p, ring(z - sg * step)]
        remote(block, block, ag_send, ag_sem.at[p, step], x * RING + ring(z + sg), cfg).start()

        @pl.when(step < 3)
        def _():
            block = qb.at[p, ring(z + sg * step)]
            remote(
                block, block, ag_send, ag_sem.at[p, 4 + step], x * RING + ring(z - sg), cfg
            ).start()

    def gather_start(p):
        wait(qb.at[p, z], q_sem.at[p])
        gather_send(p, 0)

    def gather_wait(p, step):
        sg = sign(p)
        wait(qb.at[p, ring(z - sg * (step + 1))], ag_sem.at[p, step])

        @pl.when(step < 3)
        def _():
            wait(qb.at[p, ring(z + sg * (step + 1))], ag_sem.at[p, 4 + step])

    def turn_values(p):
        vt[0:width, :] = vb[p].T

    def compute(p, j):
        sg = sign(p)
        b0 = ring(z + sg * (4 - j))
        b1 = ring(z - sg * (3 - j))
        for n, b in enumerate((b0, b1)):
            qbd[n * lanes : n * lanes + TILE, 0:HEAD] = qb[p, b, :, 0:HEAD]
            qbd[n * lanes + TILE : (n + 1) * lanes, HEAD:width] = qb[p, b, :, HEAD:width]
        top = jnp.full((1, 2 * lanes), NEG, jnp.float32)
        for s in range(6):
            part = lax.dot_general(
                kb[p, s * TILE : (s + 1) * TILE, :], qbd[...], NT,
                preferred_element_type=jnp.float32,
            )
            scores[s * TILE : (s + 1) * TILE, :] = part
            here = jnp.max(part, axis=0, keepdims=True)
            ok = jnp.concatenate([valid[b0, s : s + 1, :], valid[b1, s : s + 1, :]], axis=1)
            top = jnp.maximum(top, jnp.where(ok > 0.0, here, NEG))
        for s in range(6):
            ok = jnp.concatenate([valid[b0, s : s + 1, :], valid[b1, s : s + 1, :]], axis=1)
            shift = jnp.where(ok > 0.0, top, BIG)
            probs[s * TILE : (s + 1) * TILE, :] = jnp.exp2(
                (scores[s * TILE : (s + 1) * TILE, :] - shift) * factor
            ).astype(jnp.bfloat16)
        both = jnp.dot(vt[...], probs[...], preferred_element_type=jnp.float32)
        total = both[width : width + 1, :]
        some = total > 0.0
        safe = jnp.where(some, total, 1.0)
        lse = jnp.where(some, top * factor + jnp.log2(safe), NEG)
        scale = jnp.where(some, 1.0 / safe, 0.0)
        lane = lax.broadcasted_iota(jnp.int32, (1, 2 * lanes), 1)
        first = lax.rem(lane, lanes) < TILE
        o = jnp.where(first, both[0:HEAD, :], both[HEAD:width, :]) * scale
        slot = lax.rem(p, 3)
        for n in range(2):
            own[slot, 2 * j + n] = o[:, n * lanes : (n + 1) * lanes]
            own_lse[slot, 2 * j + n] = lse[:, n * lanes : (n + 1) * lanes]

    def merge(oa, la, ob, lb):
        m = jnp.maximum(la, lb)
        wa = jnp.exp2(la - m)
        wb = jnp.exp2(lb - m)
        t = wa + wb
        r = 1.0 / t
        return oa * (wa * r) + ob * (wb * r), m + jnp.log2(t)

    def chain_send(p, at, o, lse, to):
        stage[p, at] = o.astype(jnp.bfloat16)
        stage_lse[p, at] = lse
        there = x * RING + ring(to)
        remote(stage.at[p, at], got.at[p, at], rs_send, rs_sem.at[p, at], there, cfg).start()
        remote(
            stage_lse.at[p, at], got_lse.at[p, at], lse_send, lse_sem.at[p, at], there, cfg
        ).start()

    def chain_merge(p, at, mine):
        slot = lax.rem(p, 3)
        wait(got.at[p, at], rs_sem.at[p, at])
        wait(got_lse.at[p, at], lse_sem.at[p, at])
        return merge(
            own[slot, mine], own_lse[slot, mine], got[p, at].astype(jnp.float32), got_lse[p, at]
        )

    def reduce_send(p, step):
        sg = sign(p)
        slot = lax.rem(p, 3)

        @pl.when(step == 0)
        def _():
            chain_send(p, 0, own[slot, 0], own_lse[slot, 0], z + sg)
            chain_send(p, 4, own[slot, 1], own_lse[slot, 1], z - sg)

        @pl.when(step > 0)
        def _():
            o, lse = chain_merge(p, step - 1, 2 * step)
            chain_send(p, step, o, lse, z + sg)

        @pl.when((step > 0) & (step < 3))
        def _():
            o, lse = chain_merge(p, 3 + step, 2 * step + 1)
            chain_send(p, 4 + step, o, lse, z - sg)

    def finish(p):
        slot = lax.rem(p, 3)
        o = own[slot, 7]
        lse = own_lse[slot, 7]
        for at in (6, 3):
            wait(got.at[p, at], rs_sem.at[p, at])
            wait(got_lse.at[p, at], lse_sem.at[p, at])
            o, lse = merge(o, lse, got[p, at].astype(jnp.float32), got_lse[p, at])
        turned = o.T.astype(jnp.bfloat16)
        g = lax.div(p, 2)
        e = lax.rem(p, 2)
        for c in range(8):
            att[g, e * 8 + c] = turned[c * 48 : (c + 1) * 48, :]

    def share(c):
        lo = lax.rem(hx + lax.rem(lax.div(c, 2), 2), 2)
        return lo, lax.div(c, 4) * 4 + (1 - lo) * 2 + lax.rem(c, 2)

    def spread(p):
        g = lax.div(p, 2)
        e = lax.rem(p, 2)
        for step in range(members // 2):
            c = e * (members // 2) + lax.rem(cfg + step, members // 2)
            lo, which = share(c)

            @pl.when(c == cfg)
            def _():
                pltpu.make_async_copy(att.at[g, which], comb.at[g, cfg], comb_sem.at[g]).start()

            @pl.when(c != cfg)
            def _():
                remote(
                    att.at[g, which], comb.at[g, cfg], att_send, comb_sem.at[g], lo * RING + z, c
                ).start()

    def combine(g):
        wait(comb.at[g], comb_sem.at[g])
        sel[...] = comb[g]
        for m in range(members):
            a = sel[m].astype(jnp.float32)
            other = sel[partner[m]].astype(jnp.float32)
            gst[g, m] = (other + strength[m] * (a - other)).astype(jnp.bfloat16)

    def give(g):
        hh = lax.div(cfg, 4)
        start = pl.multiple_of(lax.rem(cfg, 2) * 48, 16)
        cols = pl.ds(pl.multiple_of(hx * half + g * 2 * width + hh * HEAD, HEAD), HEAD)
        for step in range(members):
            m = lax.rem(cfg + step, members)
            remote(
                gst.at[g, m], out.at[0, pl.ds(start, 48), cols], gst_send, out_sem,
                ox * RING + z, m,
            ).start()

    def body(u, carry):
        t = u - LEAD
        i = lax.div(t + 16, 4) - 4
        j = lax.rem(t + 16, 4)
        hop = lax.rem(4 - j, 4)
        back = lax.div(t - 3 * hop + 32, 4) - 8
        ahead = back + 3
        now = (i >= 0) & (i < pairs)

        @pl.when((hop > 0) & (ahead >= 0) & (ahead < pairs))
        def _():
            gather_wait(ahead, hop - 1)
            gather_send(ahead, hop)

        @pl.when((hop == 0) & (ahead + 1 < pairs))
        def _():
            gather_start(ahead + 1)

        @pl.when(j == 0)
        def _():
            @pl.when(now)
            def _():
                wait(kb.at[i], k_sem.at[i])
                wait(vb.at[i], v_sem.at[i])

            @pl.when((i >= 1 - DEPTH) & (i + DEPTH < pairs))
            def _():
                swap_kv(i + DEPTH)

            @pl.when(now)
            def _():
                gather_wait(i, 3)
                turn_values(i)

        active = (back >= 0) & (back < pairs)

        @pl.when(now)
        def _():
            compute(i, j)

        @pl.when(active)
        def _():
            reduce_send(back, hop)

        @pl.when((j == 0) & (i >= 3) & (i - 3 < pairs))
        def _():
            finish(i - 3)
            spread(i - 3)

        @pl.when((t >= 19) & (lax.rem(t + 32 - 19, 8) == 0))
        def _():
            combine(lax.div(t - 19, 8))

        last = 4 * pairs
        for g, slot in enumerate((last, last + 1, last + 3, last + 11)):

            @pl.when(t == slot)
            def _():
                give(g)

        return carry

    gather_start(0)
    lax.fori_loop(0, LEAD + 4 * (pairs - 1) + 16, body, 0)

    wait(out.at[0], out_sem)
    wait(kb.at[:, 0:rows], ks_send)
    wait(vb.at[:, 0:rows], vs_send)
    wait(qb.at[:, 0, 0:qrows], qs_send)
    wait(qb.at[:, 0:7], ag_send)
    wait(stage, rs_send)
    wait(stage_lse, lse_send)
    wait(att.at[:, 0 : members - 1], att_send)
    wait(gst, gst_send)


def body(query_states, key_states, value_states, tile_pattern, strength, partner):
    rows = key_states.shape[1]
    qrows = query_states.shape[1]
    pairs = query_states.shape[2] // (4 * HEAD)
    members = lax.axis_size("cfg")
    width, lanes = 2 * HEAD, 2 * TILE
    bf, f32 = jnp.bfloat16, jnp.float32
    vm = pltpu.VMEM
    dma = pltpu.SemaphoreType.DMA
    return pl.pallas_call(
        kernel,
        out_shape=jax.ShapeDtypeStruct(query_states.shape, bf),
        in_specs=[
            pl.BlockSpec(memory_space=pltpu.VMEM),
            pl.BlockSpec(memory_space=pltpu.SMEM),
            pl.BlockSpec(memory_space=pltpu.SMEM),
            pl.BlockSpec(memory_space=pl.ANY),
            pl.BlockSpec(memory_space=pl.ANY),
            pl.BlockSpec(memory_space=pl.ANY),
        ],
        out_specs=pl.BlockSpec(memory_space=pl.ANY),
        scratch_shapes=[
            vm((pairs, 2 * rows, width), bf),
            vm((pairs, 2 * rows, width), bf),
            vm((pairs, RING, 2 * qrows, width), bf),
            vm((2 * lanes, width), bf),
            vm((width + 16, 2 * rows), bf),
            vm((2 * rows, 2 * lanes), f32),
            vm((2 * rows, 2 * lanes), bf),
            vm((RING, 8, lanes), f32),
            vm((3, 8, HEAD, lanes), f32),
            vm((3, 8, 1, lanes), f32),
            vm((pairs, 7, HEAD, lanes), bf),
            vm((pairs, 7, 1, lanes), f32),
            vm((pairs, 7, HEAD, lanes), bf),
            vm((pairs, 7, 1, lanes), f32),
            vm((pairs // 2, members, 48, HEAD), bf),
            vm((pairs // 2, members, 48, HEAD), bf),
            vm((members, 48, HEAD), bf),
            vm((pairs // 2, members, 48, HEAD), bf),
            dma((pairs,)),
            dma((pairs,)),
            dma((pairs,)),
            dma((pairs, 7)),
            dma((pairs, 7)),
            dma((pairs, 7)),
            dma((pairs // 2,)),
            dma,
            dma,
            dma,
            dma,
            dma,
            dma,
            dma,
            dma,
            dma,
        ],
        compiler_params=pltpu.CompilerParams(
            collective_id=0, has_side_effects=True, vmem_limit_bytes=60 * 1024 * 1024
        ),
        cost_estimate=pl.CostEstimate(
            flops=30_000_000_000, bytes_accessed=24_000_000, transcendentals=28_000_000
        ),
    )(tile_pattern, strength, partner, query_states, key_states, value_states)


def solution(mesh):
    return jax.shard_map(
        body,
        mesh=mesh,
        in_specs=(
            P("cfg", "seq", None),
            P("cfg", "seq", None),
            P("cfg", "seq", None),
            P(),
            P(),
            P(),
        ),
        out_specs=P("cfg", "seq", None),
        check_vma=False,
    )
```
